128 devices in a mesh: patch: 8 (over z, x_lo), head: 16 (over x_hi, y, core).
Axes of the slice: x: 4 (x_hi: 2, x_lo: 2; x = x_hi * 2 + x_lo), y: 4, z: 4, core: 2. Of those that a mesh axis runs over, the one named last changes fastest.
Arguments:
- fresh_qkv: bfloat16 [16384, 3, 2048], P(('patch', 'head')), may hold values from -20 to 20
- stale_kv: bfloat16 [16384, 2, 2048], P(('patch', 'head')), may hold values from -20 to 20
- out_weight: bfloat16 [2048, 3072], replicated, may hold values from -0.375 to 0.375
Outputs:
- mixed: bfloat16 [16384, 3072], P(('patch', 'head'))
The draws below stay inside these ranges and needn't reach their ends.
All inputs are finite; a program needn't handle non-finite values.
Results may differ from the reference program's by a relative error of at most 0.0095.
Values may be sent and summed in bfloat16 or wider, within the bound.
A program may use at most 128 MiB of HBM per device.

```python
import jax
import jax.numpy as jnp
from jax import lax

D = 3072
HEADS = 16
HEAD_DIM = 128
PATCH_TOK = 2048
TOKENS = 16384
N_PATCH = 8


def drawn_values(key, count):
    return 1.6 * jax.random.truncated_normal(key, -4.0, 4.0, (TOKENS, count, HEADS * HEAD_DIM), jnp.float32)


def draw_fresh_qkv(key, part):
    key = jax.random.fold_in(key, 11)
    values = drawn_values(key, 3)
    return values.astype(jnp.bfloat16)


def draw_stale_kv(key, part):
    key = jax.random.fold_in(key, 12)
    values = drawn_values(key, 2)
    return values.astype(jnp.bfloat16)


def normal_values(stream_key, dims, scale, bound, kind=jnp.bfloat16):
    values = jax.random.normal(stream_key, dims, jnp.float32) * scale
    return jnp.minimum(jnp.maximum(values, -bound), bound).astype(kind)


def setup_inputs(seed: int = 0) -> dict:
    key_of = jax.random.split(jax.random.key(seed), 4)
    fresh_qkv = draw_fresh_qkv(jax.random.fold_in(key_of[3], 71), 0)
    stale_kv = draw_stale_kv(jax.random.fold_in(key_of[3], 71), 0)
    out_weight = normal_values(key_of[2], (HEADS * HEAD_DIM, D), (HEADS * HEAD_DIM // 8) ** -0.5, 0.375)
    return {"fresh_qkv": fresh_qkv, "stale_kv": stale_kv, "out_weight": out_weight}


def attend_head(queries, keys, values):
    scores = jnp.dot(queries, keys.T, preferred_element_type=jnp.float32) * (HEAD_DIM ** -0.5)
    peak = jnp.max(scores, axis=1, keepdims=True)
    expo = jnp.exp(scores - peak)
    total = jnp.sum(expo, axis=1, keepdims=True)
    weights = expo.astype(jnp.bfloat16)
    return jnp.dot(weights, values, preferred_element_type=jnp.float32) / total


def reference(fresh_qkv, stale_kv, out_weight):
    width = HEADS * HEAD_DIM

    def per_patch(index):
        start = (index * PATCH_TOK).astype(jnp.int32)
        fresh_rows = lax.dynamic_slice_in_dim(fresh_qkv, start, PATCH_TOK, 0)
        merged = lax.dynamic_update_slice_in_dim(stale_kv, fresh_rows[:, 1:3, :], start, 0)
        queries = fresh_rows[:, 0, :].reshape(PATCH_TOK, HEADS, HEAD_DIM).transpose(1, 0, 2)
        keys = merged[:, 0, :].reshape(TOKENS, HEADS, HEAD_DIM).transpose(1, 0, 2)
        values = merged[:, 1, :].reshape(TOKENS, HEADS, HEAD_DIM).transpose(1, 0, 2)
        heads_out = lax.map(lambda trio: attend_head(trio[0], trio[1], trio[2]), (queries, keys, values))
        return heads_out.transpose(1, 0, 2).reshape(PATCH_TOK, width).astype(jnp.bfloat16)

    attended = lax.map(per_patch, jnp.arange(N_PATCH, dtype=jnp.int32)).reshape(TOKENS, width)
    return jnp.dot(attended, out_weight, preferred_element_type=jnp.float32).astype(jnp.bfloat16)
```

```python
import jax
import jax.numpy as jnp
from jax import lax
from jax.experimental import pallas as pl
from jax.experimental.pallas import tpu as pltpu
from jax.sharding import PartitionSpec as P

MESH = pl.DeviceIdType.MESH
BLK = 128
STEP = 512
QB = 1024
FACTOR = float(128 ** -0.5 * 1.4426950408889634)
F32 = jnp.float32
BF16 = jnp.bfloat16


def kernel(fresh, stale, weight, out,
           wbuf, send_s, send_f, kv, qbuf, acc_s, m_s, l_s, sbuf, po, pml, po_in, pml_in, a_out, a_in,
           w_sem, q_send, q_recv, qx_send, qx_recv, s_send, s_recv, f_send, f_recv,
           up_send, up_recv, dn_send, dn_recv, up2_send, up2_recv, dn2_send, dn2_recv,
           po_send, po_recv, pml_send, pml_recv, a_send, a_recv, own_sem):
    p, hd = lax.axis_index("patch"), lax.axis_index("head")
    z, xl = p // 2, p % 2
    xh, j = hd // 8, hd % 8
    me = xl * 8 + j
    my_head = (xl + xh - 2 * xl * xh) * 8 + j
    above = (2 * ((z + 1) % 4) + xl, hd)
    below = (2 * ((z + 3) % 4) + xl, hd)
    partner = (2 * z + 1 - xl, (1 - xh) * 8 + j)

    def member(t):
        tl, tj = t // 8, t % 8
        return (2 * z + tl, xh * 8 + tj), (tl + xh - 2 * tl * xh) * 8 + tj

    def remote(src, dst, send, recv, to):
        return pltpu.make_async_remote_copy(
            src_ref=src, dst_ref=dst, send_sem=send, recv_sem=recv, device_id=to, device_id_type=MESH)

    def wait_bytes(ref, sem):
        pltpu.make_async_copy(ref, ref, sem).wait()

    barrier = pltpu.get_barrier_semaphore()

    def greet(d, c):
        to, _ = member((me + d) % 16)
        pl.semaphore_signal(barrier, inc=1, device_id=to, device_id_type=MESH)
        return c

    lax.fori_loop(1, 16, greet, 0)
    for to in (above, below, partner):
        pl.semaphore_signal(barrier, inc=1, device_id=to, device_id_type=MESH)

    weight_copy = pltpu.make_async_copy(weight, wbuf, w_sem)

    def pack(source, k_row, buf):
        for h in range(16):
            cols = slice(h * BLK, (h + 1) * BLK)
            buf[h, 0] = source[k_row, :, cols]
            buf[h, 1] = source[k_row + 1, :, cols].T

    pack(stale, 0, send_s)
    pl.semaphore_wait(barrier, 18)

    def lane(h):
        return pl.ds(pl.multiple_of(h * BLK, BLK), BLK)

    def send_q(d, c):
        to, h = member((me + d) % 16)
        remote(fresh.at[0, :, lane(h)], qbuf.at[0, xl, j], q_send, q_recv, to).start()
        return c

    lax.fori_loop(1, 16, send_q, 0)
    pltpu.make_async_copy(fresh.at[0, :, lane(my_head)], qbuf.at[0, xl, j], q_recv).start()

    def send_stale(d, c):
        to, h = member((me + d) % 16)
        remote(send_s.at[h], kv.at[2 * z + xl, j], s_send, s_recv.at[me], to).start()
        return c

    lax.fori_loop(1, 16, send_stale, 0)
    pltpu.make_async_copy(send_s.at[my_head], kv.at[2 * z + xl, j], s_recv.at[me]).start()

    pack(fresh, 1, send_f)

    def send_fresh(d, c):
        to, h = member((me + d) % 16)
        remote(send_f.at[h], kv.at[8 + xl, j], f_send, f_recv, to).start()
        return c

    lax.fori_loop(1, 16, send_fresh, 0)
    pltpu.make_async_copy(send_f.at[my_head], kv.at[8 + xl, j], f_recv).start()
    weight_copy.start()

    wait_bytes(qbuf.at[0], q_recv)
    qx = remote(qbuf.at[0], qbuf.at[1], qx_send, qx_recv, partner)
    qx.start()

    def forward(i, c):
        t = (me + 16 - i) % 16
        slot = kv.at[2 * z + t // 8, t % 8]
        wait_bytes(slot, s_recv.at[t])
        remote(slot, slot, up_send, up_recv.at[t], above).start()
        remote(slot, slot, dn_send, dn_recv.at[t], below).start()
        return c

    lax.fori_loop(0, 16, forward, 0)

    def scores(qb, slab, half):
        keys = kv[slab, half * 4:half * 4 + 4, 0].reshape(STEP, BLK)
        queries = qbuf[qb // 2, qb % 2].reshape(QB, BLK)
        return lax.dot_general(keys, queries, (((1,), (1,)), ((), ())), preferred_element_type=F32)

    def weighted(slab, half, weights):
        values = jnp.concatenate([kv[slab, half * 4 + c, 1] for c in range(4)], axis=1)
        return jnp.dot(values, weights, preferred_element_type=F32)

    def phase(order, count, slabs, first, finish):
        steps = [(slab, half) for slab in slabs for half in range(2)]
        sbuf[...] = scores(order(0), steps[0][0](order(0)), steps[0][1])

        def block(i, c):
            qb = order(i)
            following = order(jnp.minimum(i + 1, count - 1))
            if not first:
                m, l, acc = m_s[qb, 0:1], l_s[qb, 0:1], acc_s[qb]
            s = sbuf[...]
            for n, (slab, half) in enumerate(steps):
                if n + 1 < len(steps):
                    upcoming = scores(qb, steps[n + 1][0](qb), steps[n + 1][1])
                else:
                    sbuf[...] = scores(following, steps[0][0](following), steps[0][1])
                peak = jnp.max(s, axis=0, keepdims=True) * FACTOR
                if first and n == 0:
                    m = peak
                    w = jnp.exp2(s * FACTOR - m)
                    l = jnp.sum(w, axis=0, keepdims=True)
                    acc = weighted(slab(qb), half, w.astype(BF16))
                else:
                    new = jnp.maximum(m, peak)
                    shrink = jnp.exp2(m - new)
                    m = new
                    w = jnp.exp2(s * FACTOR - m)
                    l = l * shrink + jnp.sum(w, axis=0, keepdims=True)
                    acc = acc * shrink + weighted(slab(qb), half, w.astype(BF16))
                s = upcoming
            if finish is None:
                m_s[qb, 0:1], l_s[qb, 0:1], acc_s[qb] = m, l, acc
            else:
                finish(qb, m, l, acc)
            return c

        lax.fori_loop(0, count, block, 0)

    qx.wait_recv()
    phase(lambda i: i, 4, [lambda qb: 2 * z + 1 - qb % 2], True, None)

    zb, za, zo = (z + 3) % 4, (z + 1) % 4, (z + 2) % 4

    def forward_up(t, c):
        slot = kv.at[2 * zb, t]
        wait_bytes(slot, up_recv.at[t])
        remote(slot, slot, up2_send, up2_recv, above).start()
        return c

    def forward_dn(t, c):
        slot = kv.at[2 * za + 1, t]
        wait_bytes(slot, dn_recv.at[8 + t])
        remote(slot, slot, dn2_send, dn2_recv, below).start()
        return c

    wait_bytes(kv.at[pl.ds(8, 2)], f_recv)
    phase(lambda i: i, 4, [lambda qb: 8 + qb % 2], False, None)

    lax.fori_loop(0, 8, forward_up, 0)
    lax.fori_loop(0, 8, forward_dn, 0)

    def rest_up(t, c):
        wait_bytes(kv.at[2 * zb + 1, t], up_recv.at[8 + t])
        wait_bytes(kv.at[2 * za, t], dn_recv.at[t])
        return c

    lax.fori_loop(0, 8, rest_up, 0)
    phase(lambda i: i, 4,
          [lambda qb: 2 * zb, lambda qb: 2 * za + 1, lambda qb: 2 * zb + 1, lambda qb: 2 * za], False, None)

    wait_bytes(kv.at[2 * zo], up2_recv)
    wait_bytes(kv.at[2 * zo + 1], dn2_recv)
    far = [lambda qb: 2 * zo, lambda qb: 2 * zo + 1]

    def hand_over(qb, m, l, acc):
        pb = qb % 2
        po[pb] = (acc / l).astype(BF16)
        pml[pb, 0:4] = jnp.broadcast_to(m, (4, QB))
        pml[pb, 4:8] = jnp.broadcast_to(l, (4, QB))
        remote(po.at[pb], po_in.at[pb], po_send.at[pb], po_recv.at[pb], partner).start()
        remote(pml.at[pb], pml_in.at[pb], pml_send.at[pb], pml_recv.at[pb], partner).start()

    def combine(qb, m, l, acc):
        pb = qb % 2
        wait_bytes(po_in.at[pb], po_recv.at[pb])
        wait_bytes(pml_in.at[pb], pml_recv.at[pb])
        m2, l2 = pml_in[pb, 0:1], pml_in[pb, 4:5]
        top = jnp.maximum(m, m2)
        mine, other = jnp.exp2(m - top), jnp.exp2(m2 - top) * l2
        total = l * mine + other
        both = (acc * mine + po_in[pb].astype(F32) * other) / total
        a_out[pb] = both.T.astype(BF16).reshape(8, BLK, BLK)

        def give(d, c):
            t = (j + d) % 8
            to = (2 * z + pb, xh * 8 + t)

            @pl.when(pb * 8 + t != me)
            def _():
                remote(a_out.at[pb, t], a_in.at[my_head], a_send, a_recv, to).start()

            @pl.when(pb * 8 + t == me)
            def _():
                pltpu.make_async_copy(a_out.at[pb, t], a_in.at[my_head], a_recv).start()

            return c

        lax.fori_loop(0, 8, give, 0)

    phase(lambda i: 2 + i, 2, far, False, hand_over)
    phase(lambda i: i, 2, far, False, combine)

    weight_copy.wait()
    wait_bytes(a_in, a_recv)
    rows = jnp.concatenate([a_in[h] for h in range(16)], axis=1)

    def project(n, c):
        cols = pl.ds(pl.multiple_of(n * 512, 512), 512)
        out[:, cols] = jnp.dot(rows, wbuf[:, cols], preferred_element_type=F32).astype(BF16)
        return c

    lax.fori_loop(0, 6, project, 0)

    wait_bytes(qbuf.at[0, 0], qx_send)
    wait_bytes(qbuf.at[0, 1], qx_send)
    wait_bytes(a_out.at[0], up2_send)
    wait_bytes(a_out.at[0], up2_send)
    wait_bytes(a_out.at[0], dn2_send)
    wait_bytes(a_out.at[0], dn2_send)
    wait_bytes(send_s, up_send)
    wait_bytes(send_s, dn_send)
    wait_bytes(a_in.at[pl.ds(0, 15)], q_send)
    wait_bytes(a_in.at[pl.ds(0, 15)], a_send)
    wait_bytes(send_s.at[pl.ds(0, 15)], s_send)
    wait_bytes(send_s.at[pl.ds(0, 15)], f_send)
    for pb in range(2):
        wait_bytes(po.at[pb], po_send.at[pb])
        wait_bytes(pml.at[pb], pml_send.at[pb])


def on_device(fresh_qkv, stale_kv, out_weight):
    fresh, stale = jnp.transpose(fresh_qkv, (1, 0, 2)), jnp.transpose(stale_kv, (1, 0, 2))
    vmem = pl.BlockSpec(memory_space=pltpu.VMEM)
    dma = pltpu.SemaphoreType.DMA
    rows, width = fresh.shape[1], out_weight.shape[1]
    return pl.pallas_call(
        kernel,
        out_shape=jax.ShapeDtypeStruct((rows, width), BF16),
        in_specs=[vmem, vmem, pl.BlockSpec(memory_space=pl.ANY)],
        out_specs=vmem,
        scratch_shapes=[
            pltpu.VMEM(out_weight.shape, BF16),
            pltpu.VMEM((16, 2, BLK, BLK), BF16),
            pltpu.VMEM((16, 2, BLK, BLK), BF16),
            pltpu.VMEM((10, 8, 2, BLK, BLK), BF16),
            pltpu.VMEM((2, 2, 8, BLK, BLK), BF16),
            pltpu.VMEM((4, BLK, QB), F32),
            pltpu.VMEM((4, 8, QB), F32),
            pltpu.VMEM((4, 8, QB), F32),
            pltpu.VMEM((STEP, QB), F32),
            pltpu.VMEM((2, BLK, QB), BF16),
            pltpu.VMEM((2, 8, QB), F32),
            pltpu.VMEM((2, BLK, QB), BF16),
            pltpu.VMEM((2, 8, QB), F32),
            pltpu.VMEM((2, 8, BLK, BLK), BF16),
            pltpu.VMEM((16, BLK, BLK), BF16),
            dma, dma, dma, dma, dma, dma, dma((16,)), dma, dma,
            dma, dma((16,)), dma, dma((16,)), dma, dma, dma, dma,
            dma((2,)), dma((2,)), dma((2,)), dma((2,)), dma, dma, dma,
        ],
        compiler_params=pltpu.CompilerParams(
            collective_id=0, has_side_effects=True, vmem_limit_bytes=60 * 2 ** 20),
        cost_estimate=pl.CostEstimate(flops=19 * 10 ** 9, bytes_accessed=16 * 2 ** 20, transcendentals=2 ** 25),
    )(fresh, stale, out_weight)


def solution(mesh):
    return jax.shard_map(
        on_device,
        mesh=mesh,
        in_specs=(P(("patch", "head"), None, None), P(("patch", "head"), None, None), P()),
        out_specs=P(("patch", "head"), None),
        check_vma=False,
    )
```

```python
import jax
import jax.numpy as jnp
from jax import lax
from jax.experimental import pallas as pl
from jax.experimental.pallas import tpu as pltpu
from jax.sharding import PartitionSpec as P

MESH = pl.DeviceIdType.MESH
BLK = 128
QUAD = 4 * BLK
QB = 512
MAX_KEYS = 1024
FACTOR = float(128 ** -0.5 * 1.4426950408889634)
F32 = jnp.float32
BF16 = jnp.bfloat16


def kernel(fresh, stale_in, weight, out,
           stale, keep, wbuf, send_s, send_f, kv, qbuf, acc_s, m_s, sbuf, po, pml, po_in, pml_in, a_out, a_in,
           in_sem, w_sem, q_send, q_recv, qx_send, qx_recv, s_send, s_recv, f_send, f_recv,
           up_send, up_recv, dn_send, dn_recv, up2_send, up2_recv, dn2_send, dn2_recv,
           po_send, po_recv, pml_send, pml_recv, a_send, a_recv):
    p, hd = lax.axis_index("patch"), lax.axis_index("head")
    z, xl = p // 2, p % 2
    xh, j = hd // 8, hd % 8
    yh, jl = j // 4, j % 4
    me = xl * 8 + j
    my_head = (xl + xh - 2 * xl * xh) * 8 + j
    above = (2 * ((z + 1) % 4) + xl, hd)
    below = (2 * ((z + 3) % 4) + xl, hd)
    partner = (2 * z + 1 - xl, (1 - xh) * 8 + j)
    TURN = ((1, 0), (0, 1), (1, 1), (0, 0))

    def side(k):
        return (xl + TURN[k][0]) % 2, (yh + TURN[k][1]) % 2

    def quad(plane, k):
        a, b = side(k)
        return (plane * 2 + a) * 2 + b

    def remote(src, dst, send, recv, to):
        return pltpu.make_async_remote_copy(
            src_ref=src, dst_ref=dst, send_sem=send, recv_sem=recv, device_id=to, device_id_type=MESH)

    def wait_bytes(ref, sem):
        pltpu.make_async_copy(ref, ref, sem).wait()

    def lane(h):
        return pl.ds(pl.multiple_of(h * BLK, BLK), BLK)

    def each_member(k, action):
        a, b = side(k)

        def one(d, c):
            tj = b * 4 + (jl + d) % 4
            action((2 * z + a, xh * 8 + tj), (a + xh - 2 * a * xh) * 8 + tj)
            return c

        lax.fori_loop(1 if k == 3 else 0, 4, one, 0)

    barrier = pltpu.get_barrier_semaphore()

    def greet(to, h):
        pl.semaphore_signal(barrier, inc=1, device_id=to, device_id_type=MESH)

    for k in range(4):
        each_member(k, greet)
    for to in (above, below, partner):
        greet(to, 0)

    weight_copy = pltpu.make_async_copy(weight, wbuf, w_sem)
    stale_copy = pltpu.make_async_copy(stale_in, stale, in_sem.at[0])
    fresh_copy = pltpu.make_async_copy(fresh.at[pl.ds(1, 2)], keep, in_sem.at[1])
    stale_copy.start()
    fresh_copy.start()
    stale_copy.wait()
    def pack_stale(k):
        a, b = side(k)
        for t in range(4):
            h = (a + xh - 2 * a * xh) * 8 + b * 4 + t
            pair = stale[:, :, lane(h)]
            send_s[h, 0] = pair[:, 0, :]
            send_s[h, 1] = pair[:, 1, :].T

    pack_stale(0)
    pack_stale(1)
    pl.semaphore_wait(barrier, 18)

    def send_stale(k):
        each_member(k, lambda to, h: remote(
            send_s.at[h], kv.at[quad(z, 3), jl], s_send, s_recv.at[k], to).start())

    send_stale(0)
    send_stale(1)
    for k in range(4):
        each_member(k, lambda to, h: remote(
            fresh.at[0, :, lane(h)], qbuf.at[0, xl, yh, jl], q_send, q_recv.at[k], to).start())
    pltpu.make_async_copy(fresh.at[0, :, lane(my_head)], qbuf.at[0, xl, yh, jl], q_recv.at[3]).start()

    def send_fresh(k):
        each_member(k, lambda to, h: remote(
            send_f.at[h], kv.at[16 + xl * 2 + yh, jl], f_send, f_recv, to).start())

    pack_stale(2)
    pack_stale(3)
    fresh_copy.wait()
    for h in range(16):
        cols = slice(h * BLK, (h + 1) * BLK)
        send_f[h, 0] = keep[0, :, cols]
        send_f[h, 1] = keep[1, :, cols].T

    def pass_queries(k):
        a, b = side(k)
        wait_bytes(qbuf.at[0, a, b], q_recv.at[k])
        remote(qbuf.at[0, a, b], qbuf.at[1, a, b], qx_send, qx_recv, partner).start()

    def stale_here(k):
        wait_bytes(kv.at[quad(z, k)], s_recv.at[k])

    def pass_stale(k):
        slot = kv.at[quad(z, k)]
        remote(slot, slot, up_send, up_recv.at[k], above).start()
        remote(slot, slot, dn_send, dn_recv.at[k], below).start()

    def scores(qb, quads):
        keys = jnp.concatenate([kv[q4(qb), :, 0].reshape(QUAD, BLK) for q4 in quads], axis=0)
        queries = qbuf[qb // 4, (qb // 2) % 2, qb % 2].reshape(QB, BLK)
        return lax.dot_general(keys, queries, (((1,), (1,)), ((), ())), preferred_element_type=F32)

    def weighted(qb, quads, weights):
        values = jnp.concatenate([kv[q4(qb), c, 1] for q4 in quads for c in range(4)], axis=1)
        values = jnp.concatenate([values, jnp.ones((16, values.shape[1]), BF16)], axis=0)
        return jnp.dot(values, weights, preferred_element_type=F32)

    def phase(order, count, steps, first=False, finish=None, per=1):
        height = len(steps[0]) * QUAD
        ahead = sbuf.at[pl.ds(0, height)]
        ahead[...] = scores(order(0), steps[0])

        def group(g, c):
            work = [(u, n) for u in range(per) for n in range(len(steps))]
            blocks = [order(g * per + u) for u in range(per)]
            following = order(jnp.minimum((g + 1) * per, count - 1))
            s = ahead[...]
            behind = None

            def settle(behind):
                u, n, w, shrink, acc = behind
                part = weighted(blocks[u], steps[n], w)
                return part if acc is None else acc * shrink + part

            def store(u, m, acc):
                if finish is None:
                    m_s[blocks[u], 0:1], acc_s[blocks[u]] = m, acc
                else:
                    finish(blocks[u], m, acc[BLK:BLK + 1], acc[:BLK])

            for at_work, (u, n) in enumerate(work):
                qb = blocks[u]
                if at_work + 1 < len(work):
                    u2, n2 = work[at_work + 1]
                    upcoming = scores(blocks[u2], steps[n2])
                elif count > per:
                    ahead[...] = scores(following, steps[0])
                if n == 0:
                    before, acc = (None, None) if first else (m_s[qb, 0:1], acc_s[qb])
                else:
                    before = m
                if behind is not None:
                    done = settle(behind[:5])
                    if n == 0:
                        store(behind[0], behind[5], done)
                    else:
                        acc = done
                peak = jnp.max(s, axis=0, keepdims=True) * FACTOR
                m = peak if before is None else jnp.maximum(before, peak)
                shrink = None if before is None else jnp.exp2(before - m)
                w = jnp.exp2(s * FACTOR - m).astype(BF16)
                behind = (u, n, w, shrink, acc, m)
                if at_work + 1 < len(work):
                    s = upcoming
            store(behind[0], behind[5], settle(behind[:5]))
            return c

        if count > per:
            lax.fori_loop(0, count // per, group, 0)
        else:
            group(0, 0)

    def every(i):
        return i

    def own(i):
        return ((xl + i // 2) % 2) * 2 + i % 2

    def partners(i):
        return 4 + ((1 - xl) * 2 + yh + 1 + i) % 4

    def own_last(i):
        return (xl * 2 + yh + 1 + i) % 4

    def rel(qb):
        return (qb // 2 + xl) % 2

    def early(qb):
        return (z * 2 + (xl + 1 - rel(qb)) % 2) * 2 + (yh + rel(qb)) % 2

    def late(qb):
        return (z * 2 + (xl + 1 - rel(qb)) % 2) * 2 + (yh + 1 - rel(qb)) % 2

    zb, za, zo = (z + 3) % 4, (z + 1) % 4, (z + 2) % 4

    def from_below(k):
        wait_bytes(kv.at[quad(zb, k)], up_recv.at[k])

    def from_above(k):
        wait_bytes(kv.at[quad(za, k)], dn_recv.at[k])

    def on_up(k):
        slot = kv.at[quad(zb, k)]
        remote(slot, slot, up2_send, up2_recv.at[k // 2], above).start()

    def on_down(k):
        slot = kv.at[quad(za, k)]
        remote(slot, slot, dn2_send, dn2_recv.at[k // 2], below).start()

    def at(plane, k):
        return lambda qb: quad(plane, k)

    stale_here(0)
    pass_stale(0)
    stale_here(1)
    pass_stale(1)
    pass_queries(0)
    pass_queries(1)
    send_stale(2)
    send_stale(3)
    pltpu.make_async_copy(send_s.at[my_head], kv.at[quad(z, 3), jl], s_recv.at[3]).start()
    pass_queries(2)
    pass_queries(3)
    phase(own, 4, [[early]], first=True, per=4)
    from_below(0)
    from_above(0)
    phase(own, 4, [[at(zb, 0), at(za, 0)]], per=4)
    stale_here(2)
    pass_stale(2)
    stale_here(3)
    pass_stale(3)
    for k in range(4):
        send_fresh(k)
    pltpu.make_async_copy(send_f.at[my_head], kv.at[16 + xl * 2 + yh, jl], f_recv).start()
    weight_copy.start()
    on_up(0)
    from_above(1)
    on_down(1)
    from_below(1)
    phase(own, 4, [[late], [at(zb, 1), at(za, 1)]], per=4)
    wait_bytes(qbuf.at[1], qx_recv)
    phase(partners, 4, [[early, late], [at(zb, 0), at(za, 0)], [at(zb, 1), at(za, 1)]], first=True, per=2)
    from_below(2)
    on_up(2)
    from_above(3)
    on_down(3)
    from_above(2)
    from_below(3)
    wait_bytes(kv.at[pl.ds(16, 4)], f_recv)
    fresh_keys = [[lambda qb: 16 + (qb // 2 % 2) * 2, lambda qb: 17 + (qb // 2 % 2) * 2]]
    near = [[at(zb, 2), at(za, 2)], [at(zb, 3), at(za, 3)]]
    phase(partners, 4, fresh_keys + near, per=2)
    phase(own, 4, fresh_keys, per=4)

    wait_bytes(kv.at[quad(zo, 0)], up2_recv.at[0])
    wait_bytes(kv.at[quad(zo, 1)], dn2_recv.at[0])
    wait_bytes(kv.at[quad(zo, 2)], up2_recv.at[1])
    wait_bytes(kv.at[quad(zo, 3)], dn2_recv.at[1])
    far = [[at(zo, 0), at(zo, 1)], [at(zo, 2), at(zo, 3)]]

    def hand_over(qb, m, l, acc):
        pb = qb - 4
        po[pb] = (acc / l).astype(BF16)
        pml[pb, 0:4] = jnp.broadcast_to(m, (4, QB))
        pml[pb, 4:8] = jnp.broadcast_to(l, (4, QB))
        remote(po.at[pb], po_in.at[pb], po_send.at[pb], po_recv.at[pb], partner).start()
        remote(pml.at[pb], pml_in.at[pb], pml_send.at[pb], pml_recv.at[pb], partner).start()

    def combine(qb, m, l, acc):
        wait_bytes(po_in.at[qb], po_recv.at[qb])
        wait_bytes(pml_in.at[qb], pml_recv.at[qb])
        m2, l2 = pml_in[qb, 0:1], pml_in[qb, 4:5]
        top = jnp.maximum(m, m2)
        mine, other = jnp.exp2(m - top), jnp.exp2(m2 - top) * l2
        scale = 1.0 / (l * mine + other)
        both = acc * (mine * scale) + po_in[qb].astype(F32) * (other * scale)
        a_out[qb] = both.astype(BF16).T.reshape(4, BLK, BLK)

        for d in range(4):
            t = (jl + d) % 4
            if d == 0 and len(combined) == 3:
                pltpu.make_async_copy(a_out.at[qb, t], a_in.at[my_head], a_recv).start()
            else:
                remote(a_out.at[qb, t], a_in.at[my_head], a_send, a_recv,
                       (2 * z + qb // 2, xh * 8 + (qb % 2) * 4 + t)).start()
        combined.append(qb)

    combined = []
    phase(partners, 4, far, finish=hand_over, per=4)
    phase(own_last, 4, near + far, finish=combine, per=4)

    weight_copy.wait()
    wait_bytes(a_in, a_recv)
    rows = jnp.concatenate([a_in[h] for h in range(16)], axis=1)

    def project(n, c):
        cols = pl.ds(pl.multiple_of(n * 512, 512), 512)
        out[:, cols] = jnp.dot(rows, wbuf[:, cols], preferred_element_type=F32).astype(BF16)
        return c

    lax.fori_loop(0, 6, project, 0)

    wait_bytes(qbuf.at[0], qx_send)
    wait_bytes(kv.at[pl.ds(0, 4)], up_send)
    wait_bytes(kv.at[pl.ds(0, 4)], dn_send)
    wait_bytes(kv.at[pl.ds(0, 2)], up2_send)
    wait_bytes(kv.at[pl.ds(0, 2)], dn2_send)
    wait_bytes(a_in.at[pl.ds(0, 15)], q_send)
    wait_bytes(a_in.at[pl.ds(0, 15)], a_send)
    wait_bytes(send_s.at[pl.ds(0, 15)], s_send)
    wait_bytes(send_s.at[pl.ds(0, 15)], f_send)
    for pb in range(4):
        wait_bytes(po.at[pb], po_send.at[pb])
        wait_bytes(pml.at[pb], pml_send.at[pb])


def on_device(fresh_qkv, stale_kv, out_weight):
    fresh, stale = jnp.transpose(fresh_qkv, (1, 0, 2)), stale_kv
    vmem = pl.BlockSpec(memory_space=pltpu.VMEM)
    dma = pltpu.SemaphoreType.DMA
    rows, width = fresh.shape[1], out_weight.shape[1]
    return pl.pallas_call(
        kernel,
        out_shape=jax.ShapeDtypeStruct((rows, width), BF16),
        in_specs=[pl.BlockSpec(memory_space=pl.ANY)] * 3,
        out_specs=vmem,
        scratch_shapes=[
            pltpu.VMEM(stale.shape, BF16),
            pltpu.VMEM((2,) + fresh.shape[1:], BF16),
            pltpu.VMEM(out_weight.shape, BF16),
            pltpu.VMEM((16, 2, BLK, BLK), BF16),
            pltpu.VMEM((16, 2, BLK, BLK), BF16),
            pltpu.VMEM((20, 4, 2, BLK, BLK), BF16),
            pltpu.VMEM((2, 2, 2, 4, BLK, BLK), BF16),
            pltpu.VMEM((8, BLK + 16, QB), F32),
            pltpu.VMEM((8, 8, QB), F32),
            pltpu.VMEM((MAX_KEYS, QB), F32),
            pltpu.VMEM((4, BLK, QB), BF16),
            pltpu.VMEM((4, 8, QB), F32),
            pltpu.VMEM((4, BLK, QB), BF16),
            pltpu.VMEM((4, 8, QB), F32),
            pltpu.VMEM((4, 4, BLK, BLK), BF16),
            pltpu.VMEM((16, BLK, BLK), BF16),
            dma((2,)), dma, dma, dma((4,)), dma, dma, dma, dma((4,)), dma, dma,
            dma, dma((4,)), dma, dma((4,)), dma, dma((2,)), dma, dma((2,)),
            dma((4,)), dma((4,)), dma((4,)), dma((4,)), dma, dma,
        ],
        compiler_params=pltpu.CompilerParams(
            collective_id=0, has_side_effects=True, vmem_limit_bytes=60 * 2 ** 20),
        cost_estimate=pl.CostEstimate(flops=19 * 10 ** 9, bytes_accessed=16 * 2 ** 20, transcendentals=2 ** 25),
    )(fresh, stale, out_weight)


def solution(mesh):
    return jax.shard_map(
        on_device,
        mesh=mesh,
        in_specs=(P(("patch", "head"), None, None), P(("patch", "head"), None, None), P()),
        out_specs=P(("patch", "head"), None),
        check_vma=False,
    )
```

```python
import jax
import jax.numpy as jnp
from jax import lax
from jax.experimental import pallas as pl
from jax.experimental.pallas import tpu as pltpu
from jax.sharding import PartitionSpec as P

MESH = pl.DeviceIdType.MESH
BLK = 128
QUAD = 4 * BLK
QB = 512
MAX_KEYS = 1024
FACTOR = float(128 ** -0.5 * 1.4426950408889634)
F32 = jnp.float32
BF16 = jnp.bfloat16


def kernel(fresh, stale_in, weight, out,
           stale, keep, wbuf, send_s, send_f, kv, qbuf, acc_s, m_s, sbuf, po, pml, po_in, pml_in, a_out, a_in,
           in_sem, w_sem, q_send, q_recv, qx_send, qx_recv, s_send, s_recv, f_send, f_recv,
           up_send, up_recv, dn_send, dn_recv, up2_send, up2_recv, dn2_send, dn2_recv,
           po_send, po_recv, pml_send, pml_recv, a_send, a_recv):
    p, hd = lax.axis_index("patch"), lax.axis_index("head")
    z, xl = p // 2, p % 2
    xh, j = hd // 8, hd % 8
    yh, jl = j // 4, j % 4
    me = xl * 8 + j
    my_head = (xl + xh - 2 * xl * xh) * 8 + j
    above = (2 * ((z + 1) % 4) + xl, hd)
    below = (2 * ((z + 3) % 4) + xl, hd)
    partner = (2 * z + 1 - xl, (1 - xh) * 8 + j)
    TURN = ((1, 0), (0, 1), (1, 1), (0, 0))

    def side(k):
        return (xl + TURN[k][0]) % 2, (yh + TURN[k][1]) % 2

    def quad(plane, k):
        a, b = side(k)
        return (plane * 2 + a) * 2 + b

    def remote(src, dst, send, recv, to):
        return pltpu.make_async_remote_copy(
            src_ref=src, dst_ref=dst, send_sem=send, recv_sem=recv, device_id=to, device_id_type=MESH)

    def wait_bytes(ref, sem):
        pltpu.make_async_copy(ref, ref, sem).wait()

    def lane(h):
        return pl.ds(pl.multiple_of(h * BLK, BLK), BLK)

    def each_member(k, action):
        a, b = side(k)

        def one(d, c):
            tj = b * 4 + (jl + d) % 4
            action((2 * z + a, xh * 8 + tj), (a + xh - 2 * a * xh) * 8 + tj)
            return c

        lax.fori_loop(1 if k == 3 else 0, 4, one, 0)

    barrier = pltpu.get_barrier_semaphore()

    def greet(to, h):
        pl.semaphore_signal(barrier, inc=1, device_id=to, device_id_type=MESH)

    for k in range(4):
        each_member(k, greet)
    for to in (above, below, partner):
        greet(to, 0)

    weight_copy = pltpu.make_async_copy(weight, wbuf, w_sem)
    stale_copy = pltpu.make_async_copy(stale_in, stale, in_sem.at[0])
    fresh_copy = pltpu.make_async_copy(fresh.at[pl.ds(1, 2)], keep, in_sem.at[1])
    stale_copy.start()
    fresh_copy.start()
    stale_copy.wait()
    def pack_stale(k):
        a, b = side(k)
        for t in range(4):
            h = (a + xh - 2 * a * xh) * 8 + b * 4 + t
            pair = stale[:, :, lane(h)]
            send_s[h, 0] = pair[:, 0, :]
            send_s[h, 1] = pair[:, 1, :].T

    pack_stale(0)
    pack_stale(1)
    pl.semaphore_wait(barrier, 18)

    def send_stale(k):
        each_member(k, lambda to, h: remote(
            send_s.at[h], kv.at[quad(z, 3), jl], s_send, s_recv.at[k], to).start())

    send_stale(0)
    send_stale(1)
    for k in range(4):
        each_member(k, lambda to, h: remote(
            fresh.at[0, :, lane(h)], qbuf.at[0, xl, yh, jl], q_send, q_recv.at[k], to).start())
    pltpu.make_async_copy(fresh.at[0, :, lane(my_head)], qbuf.at[0, xl, yh, jl], q_recv.at[3]).start()

    def send_fresh(k):
        each_member(k, lambda to, h: remote(
            send_f.at[h], kv.at[16 + xl * 2 + yh, jl], f_send, f_recv, to).start())

    pack_stale(2)
    pack_stale(3)
    fresh_copy.wait()
    for h in range(16):
        cols = slice(h * BLK, (h + 1) * BLK)
        send_f[h, 0] = keep[0, :, cols]
        send_f[h, 1] = keep[1, :, cols].T

    def pass_queries(k):
        a, b = side(k)
        wait_bytes(qbuf.at[0, a, b], q_recv.at[k])
        remote(qbuf.at[0, a, b], qbuf.at[1, a, b], qx_send, qx_recv, partner).start()

    def stale_here(k):
        wait_bytes(kv.at[quad(z, k)], s_recv.at[k])

    def pass_stale(k):
        slot = kv.at[quad(z, k)]
        remote(slot, slot, up_send, up_recv.at[k], above).start()
        remote(slot, slot, dn_send, dn_recv.at[k], below).start()

    def stale_here(k):
        wait_bytes(kv.at[quad(z, k)], s_recv.at[k])

    def pass_stale(k):
        slot = kv.at[quad(z, k)]
        remote(slot, slot, up_send, up_recv.at[k], above).start()
        remote(slot, slot, dn_send, dn_recv.at[k], below).start()

    zb, za, zo = (z + 3) % 4, (z + 1) % 4, (z + 2) % 4

    def from_below(k):
        wait_bytes(kv.at[quad(zb, k)], up_recv.at[k])

    def from_above(k):
        wait_bytes(kv.at[quad(za, k)], dn_recv.at[k])

    def on_up(k):
        slot = kv.at[quad(zb, k)]
        remote(slot, slot, up2_send, up2_recv.at[k // 2], above).start()

    def on_down(k):
        slot = kv.at[quad(za, k)]
        remote(slot, slot, dn2_send, dn2_recv.at[k // 2], below).start()

    NEAR_0, NEAR_1, NEAR_2, NEAR_3, FAR_A, FAR_B, SAME, FRESH = range(8)
    OWN, OTHER = 0, 4
    ROUNDS = ((OWN, NEAR_0), (OWN, SAME), (OWN, NEAR_1), (OTHER, SAME), (OTHER, NEAR_0), (OTHER, NEAR_1),
              (OTHER, FRESH), (OTHER, NEAR_2), (OTHER, NEAR_3), (OTHER, FAR_A), (OTHER, FAR_B), (OWN, FRESH))
    N_ROUNDS = len(ROUNDS)
    LATE = (0, 1, 2, 3, 6, 9)

    def pick(index, values):
        out = values[0]
        for n in range(1, len(values)):
            out = jnp.where(index == n, values[n], out)
        return out

    def item(r, u):
        block = pick(r, [where for where, _ in ROUNDS]) + u
        kind = pick(r, [what for _, what in ROUNDS])
        patch = u // 2
        same = z * 2 + 1 - patch
        first = pick(kind, [quad(zb, k) for k in range(4)] + [quad(zo, 0), quad(zo, 2), same * 2, 16 + patch * 2])
        second = pick(kind, [quad(za, k) for k in range(4)] + [quad(zo, 1), quad(zo, 3), same * 2 + 1, 17 + patch * 2])
        return block, first, second

    def scores(block, first, second):
        keys = jnp.concatenate([kv[q4, :, 0].reshape(QUAD, BLK) for q4 in (first, second)], axis=0)
        queries = qbuf[block // 4, (block // 2) % 2, block % 2].reshape(QB, BLK)
        return lax.dot_general(keys, queries, (((1,), (1,)), ((), ())), preferred_element_type=F32)

    def settle(block, first, second, weights, shrink):
        values = jnp.concatenate([kv[q4, c, 1] for q4 in (first, second) for c in range(4)], axis=1)
        values = jnp.concatenate([values, jnp.ones((16, 2 * QUAD), BF16)], axis=0)
        acc_s[block] = acc_s[block] * shrink + jnp.dot(values, weights, preferred_element_type=F32)

    def before_round(r):
        @pl.when(r == 0)
        def _():
            from_below(0)
            from_above(0)

        @pl.when(r == 1)
        def _():
            stale_here(2)
            pass_stale(2)
            stale_here(3)
            pass_stale(3)
            for k in range(4):
                send_fresh(k)
            pltpu.make_async_copy(send_f.at[my_head], kv.at[16 + xl * 2 + yh, jl], f_recv).start()
            weight_copy.start()
            on_up(0)

        @pl.when(r == 2)
        def _():
            from_above(1)
            on_down(1)
            from_below(1)

        @pl.when(r == 3)
        def _():
            wait_bytes(qbuf.at[1], qx_recv)

        @pl.when(r == 6)
        def _():
            from_below(2)
            on_up(2)
            from_above(3)
            on_down(3)
            from_above(2)
            from_below(3)
            wait_bytes(kv.at[pl.ds(16, 4)], f_recv)

        @pl.when(r == 9)
        def _():
            wait_bytes(kv.at[quad(zo, 0)], up2_recv.at[0])
            wait_bytes(kv.at[quad(zo, 1)], dn2_recv.at[0])
            wait_bytes(kv.at[quad(zo, 2)], up2_recv.at[1])
            wait_bytes(kv.at[quad(zo, 3)], dn2_recv.at[1])

    def any_of(r, values):
        found = r == values[0]
        for v in values[1:]:
            found = jnp.logical_or(found, r == v)
        return found

    def hand_over(i, c):
        block = (((1 - xl) * 2 + yh + 1 + i) % 4)
        acc, m = acc_s[4 + block], m_s[4 + block, 0:1]
        l = acc[BLK:BLK + 1]
        po[block] = (acc[:BLK] * (1.0 / l)).astype(BF16)
        pml[block, 0:4] = jnp.broadcast_to(m, (4, QB))
        pml[block, 4:8] = jnp.broadcast_to(l, (4, QB))
        remote(po.at[block], po_in.at[block], po_send.at[block], po_recv.at[block], partner).start()
        remote(pml.at[block], pml_in.at[block], pml_send.at[block], pml_recv.at[block], partner).start()
        return c

    def combine(qb, m, l, acc):
        wait_bytes(po_in.at[qb], po_recv.at[qb])
        wait_bytes(pml_in.at[qb], pml_recv.at[qb])
        m2, l2 = pml_in[qb, 0:1], pml_in[qb, 4:5]
        top = jnp.maximum(m, m2)
        mine, other = jnp.exp2(m - top), jnp.exp2(m2 - top) * l2
        scale = 1.0 / (l * mine + other)
        both = acc * (mine * scale) + po_in[qb].astype(F32) * (other * scale)
        a_out[qb] = both.astype(BF16).T.reshape(4, BLK, BLK)

        for d in range(4):
            t = (jl + d) % 4
            if d == 0 and len(combined) == 3:
                pltpu.make_async_copy(a_out.at[qb, t], a_in.at[my_head], a_recv).start()
            else:
                remote(a_out.at[qb, t], a_in.at[my_head], a_send, a_recv,
                       (2 * z + qb // 2, xh * 8 + (qb % 2) * 4 + t)).start()
        combined.append(qb)

    combined = []
    def one_round(r, c):
        before_round(r)
        items = [item(r, u) for u in range(4)]
        ahead_r = jnp.where(jnp.logical_or(any_of(r, [v - 1 for v in LATE[1:]]), r == N_ROUNDS - 1), r, r + 1)
        following = item(ahead_r, 0)

        @pl.when(any_of(r, LATE))
        def _():
            sbuf[...] = scores(*items[0])

        s = sbuf[...]
        behind = None
        for u in range(4):
            if u < 3:
                upcoming = scores(*items[u + 1])
            else:
                sbuf[...] = scores(*following)
            if behind is not None:
                settle(*behind)
            block = items[u][0]
            before = m_s[block, 0:1]
            m = jnp.maximum(before, jnp.max(s, axis=0, keepdims=True) * FACTOR)
            m_s[block, 0:1] = m
            behind = (*items[u], jnp.exp2(s * FACTOR - m).astype(BF16), jnp.exp2(before - m))
            if u < 3:
                s = upcoming
        settle(*behind)

        @pl.when(r == 10)
        def _():
            lax.fori_loop(0, 4, hand_over, 0)

        return c

    m_s[...] = jnp.full(m_s.shape, -1e30, F32)
    acc_s[...] = jnp.zeros(acc_s.shape, F32)
    stale_here(0)
    pass_stale(0)
    stale_here(1)
    pass_stale(1)
    pass_queries(0)
    pass_queries(1)
    send_stale(2)
    send_stale(3)
    pltpu.make_async_copy(send_s.at[my_head], kv.at[quad(z, 3), jl], s_recv.at[3]).start()
    pass_queries(2)
    pass_queries(3)
    lax.fori_loop(0, N_ROUNDS, one_round, 0)

    steps = [(quad(zb, 2), quad(za, 2)), (quad(zb, 3), quad(za, 3)),
             (quad(zo, 0), quad(zo, 1)), (quad(zo, 2), quad(zo, 3))]
    blocks = [(xl * 2 + yh + 1 + i) % 4 for i in range(4)]
    s = scores(blocks[0], *steps[0])
    behind = None

    def weigh(behind):
        first, second, w, shrink, acc = behind
        values = jnp.concatenate([kv[q4, c, 1] for q4 in (first, second) for c in range(4)], axis=1)
        values = jnp.concatenate([values, jnp.ones((16, 2 * QUAD), BF16)], axis=0)
        return acc * shrink + jnp.dot(values, w, preferred_element_type=F32)

    for i in range(4):
        for n in range(4):
            if n < 3:
                upcoming = scores(blocks[i], *steps[n + 1])
            elif i < 3:
                upcoming = scores(blocks[i + 1], *steps[0])
            if n == 0:
                before, acc = m_s[blocks[i], 0:1], acc_s[blocks[i]]
            else:
                before = m
            if behind is not None:
                done = weigh(behind)
                if n == 0:
                    combine(blocks[i - 1], m, done[BLK:BLK + 1], done[:BLK])
                else:
                    acc = done
            m = jnp.maximum(before, jnp.max(s, axis=0, keepdims=True) * FACTOR)
            behind = (*steps[n], jnp.exp2(s * FACTOR - m).astype(BF16), jnp.exp2(before - m), acc)
            s = upcoming
    done = weigh(behind)
    combine(blocks[3], m, done[BLK:BLK + 1], done[:BLK])

    weight_copy.wait()
    wait_bytes(a_in, a_recv)
    rows = jnp.concatenate([a_in[h] for h in range(16)], axis=1)

    def project(n, c):
        cols = pl.ds(pl.multiple_of(n * 512, 512), 512)
        out[:, cols] = jnp.dot(rows, wbuf[:, cols], preferred_element_type=F32).astype(BF16)
        return c

    lax.fori_loop(0, 6, project, 0)

    wait_bytes(qbuf.at[0], qx_send)
    wait_bytes(kv.at[pl.ds(0, 4)], up_send)
    wait_bytes(kv.at[pl.ds(0, 4)], dn_send)
    wait_bytes(kv.at[pl.ds(0, 2)], up2_send)
    wait_bytes(kv.at[pl.ds(0, 2)], dn2_send)
    wait_bytes(a_in.at[pl.ds(0, 15)], q_send)
    wait_bytes(a_in.at[pl.ds(0, 15)], a_send)
    wait_bytes(send_s.at[pl.ds(0, 15)], s_send)
    wait_bytes(send_s.at[pl.ds(0, 15)], f_send)
    for pb in range(4):
        wait_bytes(po.at[pb], po_send.at[pb])
        wait_bytes(pml.at[pb], pml_send.at[pb])


def on_device(fresh_qkv, stale_kv, out_weight):
    fresh, stale = jnp.transpose(fresh_qkv, (1, 0, 2)), stale_kv
    vmem = pl.BlockSpec(memory_space=pltpu.VMEM)
    dma = pltpu.SemaphoreType.DMA
    rows, width = fresh.shape[1], out_weight.shape[1]
    return pl.pallas_call(
        kernel,
        out_shape=jax.ShapeDtypeStruct((rows, width), BF16),
        in_specs=[pl.BlockSpec(memory_space=pl.ANY)] * 3,
        out_specs=vmem,
        scratch_shapes=[
            pltpu.VMEM(stale.shape, BF16),
            pltpu.VMEM((2,) + fresh.shape[1:], BF16),
            pltpu.VMEM(out_weight.shape, BF16),
            pltpu.VMEM((16, 2, BLK, BLK), BF16),
            pltpu.VMEM((16, 2, BLK, BLK), BF16),
            pltpu.VMEM((20, 4, 2, BLK, BLK), BF16),
            pltpu.VMEM((2, 2, 2, 4, BLK, BLK), BF16),
            pltpu.VMEM((8, BLK + 16, QB), F32),
            pltpu.VMEM((8, 8, QB), F32),
            pltpu.VMEM((MAX_KEYS, QB), F32),
            pltpu.VMEM((4, BLK, QB), BF16),
            pltpu.VMEM((4, 8, QB), F32),
            pltpu.VMEM((4, BLK, QB), BF16),
            pltpu.VMEM((4, 8, QB), F32),
            pltpu.VMEM((4, 4, BLK, BLK), BF16),
            pltpu.VMEM((16, BLK, BLK), BF16),
            dma((2,)), dma, dma, dma((4,)), dma, dma, dma, dma((4,)), dma, dma,
            dma, dma((4,)), dma, dma((4,)), dma, dma((2,)), dma, dma((2,)),
            dma((4,)), dma((4,)), dma((4,)), dma((4,)), dma, dma,
        ],
        compiler_params=pltpu.CompilerParams(
            collective_id=0, has_side_effects=True, vmem_limit_bytes=60 * 2 ** 20),
        cost_estimate=pl.CostEstimate(flops=19 * 10 ** 9, bytes_accessed=16 * 2 ** 20, transcendentals=2 ** 25),
    )(fresh, stale, out_weight)


def solution(mesh):
    return jax.shard_map(
        on_device,
        mesh=mesh,
        in_specs=(P(("patch", "head"), None, None), P(("patch", "head"), None, None), P()),
        out_specs=P(("patch", "head"), None),
        check_vma=False,
    )
```

```python
import jax
import jax.numpy as jnp
from jax import lax
from jax.experimental import pallas as pl
from jax.experimental.pallas import tpu as pltpu
from jax.sharding import PartitionSpec as P

MESH = pl.DeviceIdType.MESH
BLK = 128
QUAD = 4 * BLK
QB = 512
MAX_KEYS = 1024
FACTOR = float(128 ** -0.5 * 1.4426950408889634)
F32 = jnp.float32
BF16 = jnp.bfloat16


def kernel(fresh, stale, out,
           send_s, send_f, kv, qbuf, acc_s, m_s, sbuf, po, pml, po_in, pml_in, a_out, a_in,
           q_send, q_recv, qx_send, qx_recv, s_send, s_recv, f_send, f_recv,
           up_send, up_recv, dn_send, dn_recv, up2_send, up2_recv, dn2_send, dn2_recv,
           po_send, po_recv, pml_send, pml_recv, a_send, a_recv):
    p, hd = lax.axis_index("patch"), lax.axis_index("head")
    z, xl = p // 2, p % 2
    xh, j = hd // 8, hd % 8
    yh, jl = j // 4, j % 4
    me = xl * 8 + j
    my_head = (xl + xh - 2 * xl * xh) * 8 + j
    above = (2 * ((z + 1) % 4) + xl, hd)
    below = (2 * ((z + 3) % 4) + xl, hd)
    partner = (2 * z + 1 - xl, (1 - xh) * 8 + j)
    TURN = ((1, 0), (0, 1), (1, 1), (0, 0))

    def side(k):
        return (xl + TURN[k][0]) % 2, (yh + TURN[k][1]) % 2

    def quad(plane, k):
        a, b = side(k)
        return (plane * 2 + a) * 2 + b

    def remote(src, dst, send, recv, to):
        return pltpu.make_async_remote_copy(
            src_ref=src, dst_ref=dst, send_sem=send, recv_sem=recv, device_id=to, device_id_type=MESH)

    def wait_bytes(ref, sem):
        pltpu.make_async_copy(ref, ref, sem).wait()

    def lane(h):
        return pl.ds(pl.multiple_of(h * BLK, BLK), BLK)

    def each_member(k, action):
        a, b = side(k)

        def one(d, c):
            tj = b * 4 + (jl + d) % 4
            action((2 * z + a, xh * 8 + tj), (a + xh - 2 * a * xh) * 8 + tj)
            return c

        lax.fori_loop(1 if k == 3 else 0, 4, one, 0)

    barrier = pltpu.get_barrier_semaphore()

    def greet(to, h):
        pl.semaphore_signal(barrier, inc=1, device_id=to, device_id_type=MESH)

    for k in range(4):
        each_member(k, greet)
    for to in (above, below, partner):
        greet(to, 0)

    def pack_stale(k):
        a, b = side(k)
        for t in range(4):
            h = (a + xh - 2 * a * xh) * 8 + b * 4 + t
            pair = stale[:, :, lane(h)]
            send_s[h, 0] = pair[:, 0, :]
            send_s[h, 1] = pair[:, 1, :].T

    pack_stale(0)
    pack_stale(1)
    pl.semaphore_wait(barrier, 18)

    def send_stale(k):
        each_member(k, lambda to, h: remote(
            send_s.at[h], kv.at[quad(z, 3), jl], s_send, s_recv.at[k], to).start())

    send_stale(0)
    send_stale(1)
    for k in range(4):
        each_member(k, lambda to, h: remote(
            fresh.at[0, :, lane(h)], qbuf.at[0, xl, yh, jl], q_send, q_recv.at[k], to).start())
    pltpu.make_async_copy(fresh.at[0, :, lane(my_head)], qbuf.at[0, xl, yh, jl], q_recv.at[3]).start()

    def send_fresh(k):
        each_member(k, lambda to, h: remote(
            send_f.at[h], kv.at[16 + xl * 2 + yh, jl], f_send, f_recv, to).start())

    pack_stale(2)
    pack_stale(3)
    for h in range(16):
        cols = slice(h * BLK, (h + 1) * BLK)
        send_f[h, 0] = fresh[1, :, cols]
        send_f[h, 1] = fresh[2, :, cols].T

    def pass_queries(k):
        a, b = side(k)
        wait_bytes(qbuf.at[0, a, b], q_recv.at[k])
        remote(qbuf.at[0, a, b], qbuf.at[1, a, b], qx_send, qx_recv, partner).start()

    def stale_here(k):
        wait_bytes(kv.at[quad(z, k)], s_recv.at[k])

    def pass_stale(k):
        slot = kv.at[quad(z, k)]
        remote(slot, slot, up_send, up_recv.at[k], above).start()
        remote(slot, slot, dn_send, dn_recv.at[k], below).start()

    def stale_here(k):
        wait_bytes(kv.at[quad(z, k)], s_recv.at[k])

    def pass_stale(k):
        slot = kv.at[quad(z, k)]
        remote(slot, slot, up_send, up_recv.at[k], above).start()
        remote(slot, slot, dn_send, dn_recv.at[k], below).start()

    zb, za, zo = (z + 3) % 4, (z + 1) % 4, (z + 2) % 4

    def from_below(k):
        wait_bytes(kv.at[quad(zb, k)], up_recv.at[k])

    def from_above(k):
        wait_bytes(kv.at[quad(za, k)], dn_recv.at[k])

    def on_up(k):
        slot = kv.at[quad(zb, k)]
        remote(slot, slot, up2_send, up2_recv.at[k // 2], above).start()

    def on_down(k):
        slot = kv.at[quad(za, k)]
        remote(slot, slot, dn2_send, dn2_recv.at[k // 2], below).start()

    NEAR_0, NEAR_1, NEAR_2, NEAR_3, FAR_A, FAR_B, SAME, FRESH = range(8)
    OWN, OTHER = 0, 4
    ROUNDS = ((OWN, NEAR_0), (OWN, SAME), (OWN, NEAR_1), (OTHER, SAME), (OTHER, NEAR_0), (OTHER, NEAR_1),
              (OTHER, FRESH), (OTHER, NEAR_2), (OTHER, NEAR_3), (OTHER, FAR_A), (OTHER, FAR_B), (OWN, FRESH))
    N_ROUNDS = len(ROUNDS)
    LATE = (0, 1, 2, 3, 6, 9)

    def pick(index, values):
        out = values[0]
        for n in range(1, len(values)):
            out = jnp.where(index == n, values[n], out)
        return out

    def item(r, u):
        block = pick(r, [where for where, _ in ROUNDS]) + u
        kind = pick(r, [what for _, what in ROUNDS])
        patch = u // 2
        same = z * 2 + 1 - patch
        first = pick(kind, [quad(zb, k) for k in range(4)] + [quad(zo, 0), quad(zo, 2), same * 2, 16 + patch * 2])
        second = pick(kind, [quad(za, k) for k in range(4)] + [quad(zo, 1), quad(zo, 3), same * 2 + 1, 17 + patch * 2])
        return block, first, second

    def scores(block, first, second):
        keys = jnp.concatenate([kv[q4, :, 0].reshape(QUAD, BLK) for q4 in (first, second)], axis=0)
        queries = qbuf[block // 4, (block // 2) % 2, block % 2].reshape(QB, BLK)
        return lax.dot_general(keys, queries, (((1,), (1,)), ((), ())), preferred_element_type=F32)

    def settle(block, first, second, weights, shrink):
        values = jnp.concatenate([kv[q4, c, 1] for q4 in (first, second) for c in range(4)], axis=1)
        values = jnp.concatenate([values, jnp.ones((16, 2 * QUAD), BF16)], axis=0)
        acc_s[block] = acc_s[block] * shrink + jnp.dot(values, weights, preferred_element_type=F32)

    def before_round(r):
        @pl.when(r == 0)
        def _():
            from_below(0)
            from_above(0)

        @pl.when(r == 1)
        def _():
            stale_here(2)
            pass_stale(2)
            stale_here(3)
            pass_stale(3)
            for k in range(4):
                send_fresh(k)
            pltpu.make_async_copy(send_f.at[my_head], kv.at[16 + xl * 2 + yh, jl], f_recv).start()
            on_up(0)

        @pl.when(r == 2)
        def _():
            from_above(1)
            on_down(1)
            from_below(1)

        @pl.when(r == 3)
        def _():
            wait_bytes(qbuf.at[1], qx_recv)

        @pl.when(r == 6)
        def _():
            from_below(2)
            on_up(2)
            from_above(3)
            on_down(3)
            from_above(2)
            from_below(3)
            wait_bytes(kv.at[pl.ds(16, 4)], f_recv)

        @pl.when(r == 9)
        def _():
            wait_bytes(kv.at[quad(zo, 0)], up2_recv.at[0])
            wait_bytes(kv.at[quad(zo, 1)], dn2_recv.at[0])
            wait_bytes(kv.at[quad(zo, 2)], up2_recv.at[1])
            wait_bytes(kv.at[quad(zo, 3)], dn2_recv.at[1])

    def any_of(r, values):
        found = r == values[0]
        for v in values[1:]:
            found = jnp.logical_or(found, r == v)
        return found

    def hand_over(i, c):
        block = (((1 - xl) * 2 + yh + 1 + i) % 4)
        acc, m = acc_s[4 + block], m_s[4 + block, 0:1]
        l = acc[BLK:BLK + 1]
        po[block] = (acc[:BLK] * (1.0 / l)).astype(BF16)
        pml[block, 0:4] = jnp.broadcast_to(m, (4, QB))
        pml[block, 4:8] = jnp.broadcast_to(l, (4, QB))
        remote(po.at[block], po_in.at[block], po_send.at[block], po_recv.at[block], partner).start()
        remote(pml.at[block], pml_in.at[block], pml_send.at[block], pml_recv.at[block], partner).start()
        return c

    def combine(qb, m, l, acc):
        wait_bytes(po_in.at[qb], po_recv.at[qb])
        wait_bytes(pml_in.at[qb], pml_recv.at[qb])
        m2, l2 = pml_in[qb, 0:1], pml_in[qb, 4:5]
        top = jnp.maximum(m, m2)
        mine, other = jnp.exp2(m - top), jnp.exp2(m2 - top) * l2
        scale = 1.0 / (l * mine + other)
        both = acc * (mine * scale) + po_in[qb].astype(F32) * (other * scale)
        a_out[qb] = both.astype(BF16).T.reshape(4, BLK, BLK)

        for d in range(4):
            t = (jl + d) % 4
            if d == 0 and len(combined) == 3:
                pltpu.make_async_copy(a_out.at[qb, t], a_in.at[my_head], a_recv).start()
            else:
                remote(a_out.at[qb, t], a_in.at[my_head], a_send, a_recv,
                       (2 * z + qb // 2, xh * 8 + (qb % 2) * 4 + t)).start()
        combined.append(qb)

    combined = []
    def one_round(r, c):
        before_round(r)
        items = [item(r, u) for u in range(4)]
        ahead_r = jnp.where(jnp.logical_or(any_of(r, [v - 1 for v in LATE[1:]]), r == N_ROUNDS - 1), r, r + 1)
        following = item(ahead_r, 0)

        @pl.when(any_of(r, LATE))
        def _():
            sbuf[...] = scores(*items[0])

        s = sbuf[...]
        behind = None
        for u in range(4):
            if u < 3:
                upcoming = scores(*items[u + 1])
            else:
                sbuf[...] = scores(*following)
            if behind is not None:
                settle(*behind)
            block = items[u][0]
            before = m_s[block, 0:1]
            m = jnp.maximum(before, jnp.max(s, axis=0, keepdims=True) * FACTOR)
            m_s[block, 0:1] = m
            behind = (*items[u], jnp.exp2(s * FACTOR - m).astype(BF16), jnp.exp2(before - m))
            if u < 3:
                s = upcoming
        settle(*behind)

        @pl.when(r == 10)
        def _():
            lax.fori_loop(0, 4, hand_over, 0)

        return c

    m_s[...] = jnp.full(m_s.shape, -1e30, F32)
    acc_s[...] = jnp.zeros(acc_s.shape, F32)
    stale_here(0)
    pass_stale(0)
    stale_here(1)
    pass_stale(1)
    send_stale(2)
    send_stale(3)
    pltpu.make_async_copy(send_s.at[my_head], kv.at[quad(z, 3), jl], s_recv.at[3]).start()
    pass_queries(0)
    pass_queries(1)
    pass_queries(2)
    pass_queries(3)
    lax.fori_loop(0, N_ROUNDS, one_round, 0)

    steps = [(quad(zb, 2), quad(za, 2)), (quad(zb, 3), quad(za, 3)),
             (quad(zo, 0), quad(zo, 1)), (quad(zo, 2), quad(zo, 3))]
    blocks = [(xl * 2 + yh + 1 + i) % 4 for i in range(4)]
    s = scores(blocks[0], *steps[0])
    behind = None

    def weigh(behind):
        first, second, w, shrink, acc = behind
        values = jnp.concatenate([kv[q4, c, 1] for q4 in (first, second) for c in range(4)], axis=1)
        values = jnp.concatenate([values, jnp.ones((16, 2 * QUAD), BF16)], axis=0)
        return acc * shrink + jnp.dot(values, w, preferred_element_type=F32)

    for i in range(4):
        for n in range(4):
            if n < 3:
                upcoming = scores(blocks[i], *steps[n + 1])
            elif i < 3:
                upcoming = scores(blocks[i + 1], *steps[0])
            if n == 0:
                before, acc = m_s[blocks[i], 0:1], acc_s[blocks[i]]
            else:
                before = m
            if behind is not None:
                done = weigh(behind)
                if n == 0:
                    combine(blocks[i - 1], m, done[BLK:BLK + 1], done[:BLK])
                else:
                    acc = done
            m = jnp.maximum(before, jnp.max(s, axis=0, keepdims=True) * FACTOR)
            behind = (*steps[n], jnp.exp2(s * FACTOR - m).astype(BF16), jnp.exp2(before - m), acc)
            s = upcoming
    done = weigh(behind)
    combine(blocks[3], m, done[BLK:BLK + 1], done[:BLK])

    wait_bytes(a_in, a_recv)
    for h in range(16):
        out[:, h * BLK:(h + 1) * BLK] = a_in[h]

    wait_bytes(qbuf.at[0], qx_send)
    wait_bytes(kv.at[pl.ds(0, 4)], up_send)
    wait_bytes(kv.at[pl.ds(0, 4)], dn_send)
    wait_bytes(kv.at[pl.ds(0, 2)], up2_send)
    wait_bytes(kv.at[pl.ds(0, 2)], dn2_send)
    wait_bytes(a_in.at[pl.ds(0, 15)], q_send)
    wait_bytes(a_in.at[pl.ds(0, 15)], a_send)
    wait_bytes(send_s.at[pl.ds(0, 15)], s_send)
    wait_bytes(send_s.at[pl.ds(0, 15)], f_send)
    for pb in range(4):
        wait_bytes(po.at[pb], po_send.at[pb])
        wait_bytes(pml.at[pb], pml_send.at[pb])


def on_device(fresh_qkv, stale_kv, out_weight):
    fresh, stale = jnp.transpose(fresh_qkv, (1, 0, 2)), stale_kv
    vmem = pl.BlockSpec(memory_space=pltpu.VMEM)
    dma = pltpu.SemaphoreType.DMA
    rows = fresh.shape[1]
    attended = pl.pallas_call(
        kernel,
        out_shape=jax.ShapeDtypeStruct((rows, out_weight.shape[0]), BF16),
        in_specs=[vmem] * 2,
        out_specs=vmem,
        scratch_shapes=[
            pltpu.VMEM((16, 2, BLK, BLK), BF16),
            pltpu.VMEM((16, 2, BLK, BLK), BF16),
            pltpu.VMEM((20, 4, 2, BLK, BLK), BF16),
            pltpu.VMEM((2, 2, 2, 4, BLK, BLK), BF16),
            pltpu.VMEM((8, BLK + 16, QB), F32),
            pltpu.VMEM((8, 8, QB), F32),
            pltpu.VMEM((MAX_KEYS, QB), F32),
            pltpu.VMEM((4, BLK, QB), BF16),
            pltpu.VMEM((4, 8, QB), F32),
            pltpu.VMEM((4, BLK, QB), BF16),
            pltpu.VMEM((4, 8, QB), F32),
            pltpu.VMEM((4, 4, BLK, BLK), BF16),
            pltpu.VMEM((16, BLK, BLK), BF16),
            dma, dma((4,)), dma, dma, dma, dma((4,)), dma, dma,
            dma, dma((4,)), dma, dma((4,)), dma, dma((2,)), dma, dma((2,)),
            dma((4,)), dma((4,)), dma((4,)), dma((4,)), dma, dma,
        ],
        compiler_params=pltpu.CompilerParams(
            collective_id=0, has_side_effects=True, vmem_limit_bytes=38 * 2 ** 20),
        cost_estimate=pl.CostEstimate(flops=19 * 10 ** 9, bytes_accessed=16 * 2 ** 20, transcendentals=2 ** 25),
    )(fresh, stale)
    return jnp.dot(attended, out_weight, preferred_element_type=F32).astype(BF16)


def solution(mesh):
    return jax.shard_map(
        on_device,
        mesh=mesh,
        in_specs=(P(("patch", "head"), None, None), P(("patch", "head"), None, None), P()),
        out_specs=P(("patch", "head"), None),
        check_vma=False,
    )
```
